512 devices in a mesh: topic: 8 (over y, core), dev: 64 (over z, x).
Axes of the slice: x: 4, y: 4, z: 16, core: 2. Of those that a mesh axis runs over, the one named last changes fastest.
Arguments:
- embeddings: bfloat16 [131072, 768], P(('topic', 'dev')), may hold values from -6 to 6
- topic_ids: int32 [131072], P(('topic', 'dev')), may hold values from 0 to 3
- pair_blocks: int32 [8, 64, 64], P('topic'), may hold values from -1 to 7, as said below
Outputs:
- smoothed: bfloat16 [131072, 768], P(('topic', 'dev'))
The draws below stay inside these ranges and needn't reach their ends.
Inputs may be any that keep to these rules, and one draw needn't show every extreme that they name: pair_blocks[g, m, n] >= 0 exactly when pair_blocks[g, n, m] >= 0; pair_blocks[g, m, m] = -1.
All inputs are finite; a program needn't handle non-finite values.
Results may differ from the reference program's by a relative error of at most 0.0089.
Values may be sent and summed in bfloat16 or wider, within the bound.
A program may use at most 64 MiB of HBM per device.

```python
import jax
import jax.numpy as jnp
from jax import lax

D = 768
ROWS_DEV = 256
BLOCK = 32
NSUB = 4
GROUPS = 8
MEMBERS = 64
NBLK = 8
ROWS = 131072


def draw_pair_blocks(key, part):
    density = jax.random.randint(jax.random.fold_in(key, 11), (GROUPS, MEMBERS), 6, 15)
    chance = jax.random.randint(jax.random.fold_in(key, 12), (GROUPS, MEMBERS, MEMBERS), 0, 16)
    members_range = jnp.arange(MEMBERS, dtype=jnp.int32)
    upper_half = members_range[:, None] < members_range[None, :]
    sym_chance = jnp.where(upper_half[None], chance, jnp.swapaxes(chance, 1, 2))
    present = sym_chance < density[:, :, None] + density[:, None, :]
    present = present & (members_range[:, None] != members_range[None, :])[None]
    block_draw = jax.random.randint(jax.random.fold_in(key, 13), (GROUPS, MEMBERS, MEMBERS), 0, NBLK)
    return jnp.where(present, block_draw, -1).astype(jnp.int32)


def set_ends(entries, own_key, smallest, top_value):
    dims = entries.shape
    index_at = [jax.random.randint(jax.random.fold_in(own_key, axis), (), 0, dims[axis]) for axis in range(len(dims))]
    entries = entries.at[tuple(index_at)].set(smallest)
    longest = dims.index(max(dims))
    index_at[longest] = (index_at[longest] + 1) % dims[longest]
    return entries.at[tuple(index_at)].set(top_value)


def levels(stream_key, extent, shards, low, top_value):
    gain = 1.0
    for axis_at, shards_of in shards:
        draws = jax.random.uniform(jax.random.fold_in(jax.random.fold_in(stream_key, 6), axis_at), (shards_of,), jnp.float32, low / len(shards), top_value / len(shards))
        gain = gain * jnp.repeat(jnp.exp(draws), extent[axis_at] // shards_of).reshape((-1,) + (1,) * (len(extent) - 1 - axis_at))
    return gain


def bell_draw(rng, shape, width, most, cuts=(), held_as=jnp.bfloat16):
    level = levels(rng, shape, cuts, -0.22, 0.18) if cuts else 1.0
    drawn = jax.random.normal(rng, shape, jnp.float32) * width * level
    return jnp.minimum(jnp.maximum(drawn, -most), most).astype(held_as)


def setup_inputs(seed: int = 0) -> dict:
    arg_keys = jax.random.split(jax.random.key(seed), 4)
    embeddings = bell_draw(arg_keys[0], (ROWS, D), 1.0, 6.0, ((0, 512),))
    topic_ids = set_ends(jax.random.randint(arg_keys[1], (ROWS,), 0, NSUB), jax.random.fold_in(arg_keys[1], 1), 0, NSUB - 1).astype(jnp.int32)
    pair_blocks = draw_pair_blocks(jax.random.fold_in(arg_keys[3], 71), 0)
    return {"embeddings": embeddings, "topic_ids": topic_ids, "pair_blocks": pair_blocks}


SHARPNESS = 60.0
LEAKAGE = 0.3
EPSILON = 1e-06

def normalize(embed_rows):
    values = embed_rows.astype(jnp.float32)
    row_scale = lax.rsqrt(lax.optimization_barrier(jnp.mean(values * values, axis=-1, keepdims=True)) + EPSILON)
    return (values * row_scale).astype(jnp.bfloat16)

def kernel_tiles(left_rows, right_rows, left_topic, right_topic):
    feature_width = left_rows.shape[-1]
    scores = jnp.einsum('sid,sjd->sij', left_rows.astype(jnp.float32), right_rows.astype(jnp.float32), precision=lax.Precision.HIGHEST)
    same_topic = left_topic[:, :, None] == right_topic[:, None, :]
    factor = jnp.where(same_topic, 1.0, LEAKAGE).astype(jnp.float32)
    return (jnp.exp(scores * (SHARPNESS / feature_width)) * factor).astype(jnp.bfloat16)

def own_side(my_rows, their_rows, my_topic, their_topic, live_slot):
    weights = kernel_tiles(my_rows, their_rows, my_topic, their_topic)
    weights = weights * live_slot[:, None, None].astype(jnp.bfloat16)
    pair_sum = jnp.einsum('sij,sjd->sid', weights.astype(jnp.float32), their_rows.astype(jnp.float32), precision=lax.Precision.HIGHEST).astype(jnp.bfloat16)
    pair_total = lax.optimization_barrier(jnp.sum(weights.astype(jnp.float32), axis=2)).astype(jnp.bfloat16)
    return (pair_sum, pair_total)

def local_part(normed, topic_row):
    row_count = normed.shape[0]
    step_rows = min(512, row_count)
    block_sums = []
    block_totals = []
    for first_row in range(0, row_count, step_rows):
        left_rows = normed[first_row:first_row + step_rows]
        weights = kernel_tiles(left_rows[None], normed[None], topic_row[first_row:first_row + step_rows][None], topic_row[None])[0]
        own_row = first_row + jnp.arange(step_rows, dtype=jnp.int32)[:, None]
        keep_mask = own_row != jnp.arange(row_count, dtype=jnp.int32)[None, :]
        weights = jnp.where(keep_mask, weights, jnp.zeros_like(weights))
        block_sums.append(jnp.dot(weights, normed, preferred_element_type=jnp.float32))
        block_totals.append(lax.optimization_barrier(jnp.sum(weights.astype(jnp.float32), axis=1)))
    return (jnp.concatenate(block_sums, 0), jnp.concatenate(block_totals, 0))

def reference(embeddings, topic_ids, pair_blocks):
    normed = lax.map(normalize, embeddings.reshape(GROUPS, MEMBERS * ROWS_DEV, D))
    normed = normed.reshape(GROUPS, MEMBERS, NBLK, BLOCK, D)
    topics = topic_ids.reshape(GROUPS, MEMBERS, NBLK, BLOCK)
    peers = jnp.arange(MEMBERS, dtype=jnp.int32)
    block_ids = jnp.arange(NBLK, dtype=jnp.int32)

    def one_device(flat_index):
        group_index = flat_index // MEMBERS
        member = flat_index % MEMBERS
        slab = normed[group_index]
        slab_topic = topics[group_index]
        own_blocks = slab[member]
        own_topic = slab_topic[member]
        local_sum, local_total = local_part(own_blocks.reshape(ROWS_DEV, D), own_topic.reshape(ROWS_DEV))
        my_blocks = pair_blocks[group_index, member]
        partner_blocks = pair_blocks[group_index, :, member]
        present = my_blocks >= 0
        safe_mine = jnp.maximum(my_blocks, 0).astype(jnp.int32)
        safe_theirs = jnp.maximum(partner_blocks, 0).astype(jnp.int32)
        my_rows = own_blocks[safe_mine]
        my_topic = own_topic[safe_mine]
        their_rows = slab[peers, safe_theirs]
        their_topic = slab_topic[peers, safe_theirs]
        pair_sum, pair_total = own_side(my_rows, their_rows, my_topic, their_topic, present)
        placement = ((my_blocks[:, None] == block_ids[None, :]) & present[:, None]).astype(jnp.float32)
        remote_sum = jnp.einsum('qn,qbd->nbd', placement, pair_sum.astype(jnp.float32), precision=lax.Precision.HIGHEST).reshape(ROWS_DEV, D)
        remote_total = jnp.einsum('qn,qb->nb', placement, pair_total.astype(jnp.float32), precision=lax.Precision.HIGHEST).reshape(ROWS_DEV)
        previous_group = jnp.maximum(group_index - 1, 0)
        following_group = jnp.minimum(group_index + 1, GROUPS - 1)
        head_sum, head_total = own_side(own_blocks[0][None], normed[previous_group, member, NBLK - 1][None], own_topic[0][None], topics[previous_group, member, NBLK - 1][None], (group_index > 0)[None])
        tail_sum, tail_total = own_side(own_blocks[NBLK - 1][None], normed[following_group, member, 0][None], own_topic[NBLK - 1][None], topics[following_group, member, 0][None], (group_index < GROUPS - 1)[None])
        numer = local_sum + remote_sum
        denom = local_total + remote_total
        numer = numer.at[:BLOCK].add(head_sum[0].astype(jnp.float32))
        numer = numer.at[ROWS_DEV - BLOCK:].add(tail_sum[0].astype(jnp.float32))
        denom = denom.at[:BLOCK].add(head_total[0].astype(jnp.float32))
        denom = denom.at[ROWS_DEV - BLOCK:].add(tail_total[0].astype(jnp.float32))
        return (numer / denom[:, None]).astype(jnp.bfloat16)
    result = lax.map(one_device, jnp.arange(GROUPS * MEMBERS, dtype=jnp.int32))
    return result.reshape(ROWS, D)
```

```python
import functools

import jax
import jax.numpy as jnp
from jax import lax
from jax.experimental import pallas as pl
from jax.experimental.pallas import tpu as pltpu
from jax.sharding import PartitionSpec as P

BLOCK = 32
WIDE = 4
LANES = WIDE * BLOCK
PIECES = 2

SHARPNESS = 60.0
LEAKAGE = 0.3
EPSILON = 1e-06

MESH = pl.DeviceIdType.MESH


def full_hops(depth):
    return depth // 2 - 2


def counts(depth):
    hops = full_hops(depth)
    ring = 2 * hops * PIECES
    plane = depth - 1
    picked = 3 + 2 * hops * 3 + 2 * 6
    return ring + plane + picked + 3 + 4, picked


def kernel(depth, slabs, embed, topic, pairs, out, raw, own, groups, stage, tile, parts, planes, edges,
           mine, acc, weight_sum, local_sem, send_sem, recv_sem, *rings):
    hops = full_hops(depth)
    rows, width = own.shape
    blocks = rows // BLOCK
    me = lax.axis_index("dev")
    slab = lax.axis_index("topic")
    z, x = me // WIDE, lax.rem(me, WIDE)

    def node(dz, dx):
        return lax.rem(z + dz + depth, depth) * WIDE + lax.rem(x + dx + WIDE, WIDE)

    def neighbour(by):
        return lax.rem(slab + by + slabs, slabs)

    load = pltpu.make_async_copy(embed, raw, local_sem)
    load.start()

    barrier = pltpu.get_barrier_semaphore()
    takers = [(0, o) for o in (1, 2, 3)]
    takers += [(s, o) for s in (1, -1) for o in range(WIDE)]
    takers += [(2, 0), (2, 1), (-2, 2), (-2, 3)]
    for dz, dx in takers:
        pl.semaphore_signal(barrier, inc=1, device_id={"dev": node(-dz, -dx)}, device_id_type=MESH)
    for by in (1, -1):
        pl.semaphore_signal(barrier, inc=1, device_id={"topic": neighbour(by)}, device_id_type=MESH)

    started = []
    used = [0, 0]

    def copy(src, dst, **device):
        k = used[0]
        used[0] += 1
        c = pltpu.make_async_remote_copy(
            src_ref=src, dst_ref=dst, send_sem=send_sem.at[k], recv_sem=recv_sem.at[k],
            device_id=device, device_id_type=MESH)
        c.start()
        started.append(c)
        return c

    ids = topic[...].astype(jnp.float32)
    lane = lax.broadcasted_iota(jnp.int32, (1, LANES), 1)
    lane_part = lane // BLOCK
    of_block = lax.broadcasted_iota(jnp.int32, (blocks, rows), 0) == lax.broadcasted_iota(
        jnp.int32, (blocks, rows), 1) // BLOCK
    same_place = lax.rem(lax.broadcasted_iota(jnp.int32, (rows, LANES), 0), BLOCK) == lax.rem(
        lax.broadcasted_iota(jnp.int32, (rows, LANES), 1), BLOCK)
    tile[...] = jnp.dot(
        jnp.where(of_block, ids, 0.0).astype(jnp.bfloat16), same_place.astype(jnp.bfloat16),
        preferred_element_type=jnp.float32)
    diagonal = lax.broadcasted_iota(jnp.int32, (rows, rows), 0) == lax.broadcasted_iota(
        jnp.int32, (rows, rows), 1)
    mine[...] = jnp.dot(
        jnp.where(diagonal, ids, 0.0).astype(jnp.bfloat16), jnp.ones((rows, LANES), jnp.bfloat16),
        preferred_element_type=jnp.float32)

    load.wait()
    values = raw[...].astype(jnp.float32)
    scale = lax.rsqrt(jnp.mean(values * values, axis=-1, keepdims=True) + EPSILON)
    own[...] = (values * scale).astype(jnp.bfloat16)

    pl.semaphore_wait(barrier, len(takers) + 2)

    def ring_step(way, hop, piece):
        src = own if hop == 1 else rings[way * hops + hop - 2]
        part = pl.ds(piece * (rows // PIECES), rows // PIECES)
        return copy(src.at[part], rings[way * hops + hop - 1].at[part], dev=node(1 - 2 * way, 0))

    def pick(src, owner, takers):
        count = len(takers)
        at = lax.broadcasted_iota(jnp.int32, (count * BLOCK, rows), 0)
        wanted = jnp.full((count * BLOCK, rows), pairs[0, owner, takers[0]], jnp.int32)
        for i in range(1, count):
            wanted = jnp.where(at >= i * BLOCK, pairs[0, owner, takers[i]], wanted)
        source = jnp.maximum(wanted, 0) * BLOCK + lax.rem(at, BLOCK)
        choice = lax.broadcasted_iota(jnp.int32, (count * BLOCK, rows), 1) == source
        return jnp.dot(
            choice.astype(jnp.bfloat16), src[...], preferred_element_type=jnp.float32
        ).astype(jnp.bfloat16)

    def slot(step, way):
        return groups.at[pl.ds(pl.multiple_of(step * rows + way * LANES + x * BLOCK, BLOCK), BLOCK)]

    def picks(src, step, way, dz_owner, dz_taker, offsets):
        takers = [node(dz_taker, o) for o in offsets]
        picked = pick(src, node(dz_owner, 0), takers)
        copies = []
        for i, (o, taker) in enumerate(zip(offsets, takers)):
            block = picked[i * BLOCK:(i + 1) * BLOCK]
            if dz_taker == 0 and o == 0:
                slot(step, way)[...] = block
                continue
            spot = stage.at[pl.ds(used[1] * BLOCK, BLOCK)]
            used[1] += 1
            spot[...] = block
            copies.append(copy(spot, slot(step, way), dev=taker))
        return copies

    in_ring = {}
    for piece in range(PIECES):
        for way in (0, 1):
            in_ring[way, 1, piece] = ring_step(way, 1, piece)

    beside = [copy(tile, parts.at[x], dev=node(0, o)) for o in (1, 2, 3)]
    in_slots = {0: picks(own, 0, 0, 0, 0, range(WIDE))}
    border = [
        copy(tile, edges.at[0], topic=neighbour(1)),
        copy(tile, edges.at[1], topic=neighbour(-1)),
        copy(own.at[pl.ds(rows - BLOCK, BLOCK)], groups.at[pl.ds(LANES, BLOCK)], topic=neighbour(1)),
        copy(own.at[pl.ds(0, BLOCK)], groups.at[pl.ds(LANES + BLOCK, BLOCK)], topic=neighbour(-1)),
    ]
    parts[x] = tile[...]
    groups[pl.ds(LANES + 2 * BLOCK, 2 * BLOCK), :] = jnp.zeros((2 * BLOCK, width), jnp.bfloat16)

    row_block = lax.broadcasted_iota(jnp.int32, (rows, LANES), 0) // BLOCK

    def weigh(scores, topics, keep):
        factor = jnp.where(mine[...] == topics, 1.0, LEAKAGE)
        w = jnp.exp(scores * (SHARPNESS / width)) * factor
        return jnp.where(keep, w, 0.0).astype(jnp.bfloat16)

    def against(theirs, halves, first=False):
        scores = lax.dot_general(
            own[...], theirs, (((1,), (1,)), ((), ())), preferred_element_type=jnp.float32)
        ws = [
            weigh(scores[:, i * LANES:(i + 1) * LANES], topics, keep)
            for i, (topics, keep) in enumerate(halves)
        ]
        totals = sum(w.astype(jnp.float32) for w in ws)
        w = jnp.concatenate(ws, 1) if len(ws) > 1 else ws[0]
        sums = jnp.dot(w, theirs, preferred_element_type=jnp.float32)
        if first:
            acc[...] = sums
            weight_sum[...] = totals
        else:
            acc[...] += sums
            weight_sum[...] += totals

    def by_part(values):
        row = jnp.where(lane_part == 0, values[0], values[1])
        for j in (2, 3):
            row = jnp.where(lane_part == j, values[j], row)
        return row

    def plane_half(dz, plane):
        owners = [lax.rem(z + dz + depth, depth) * WIDE + j for j in range(WIDE)]
        theirs = by_part([pairs[0, n, me] for n in owners])
        ours = by_part([pairs[0, me, n] for n in owners])
        at = lax.broadcasted_iota(jnp.int32, (blocks, LANES), 0)
        topics = jnp.sum(jnp.where(at == theirs, planes[plane], 0.0), axis=0, keepdims=True)
        return topics, row_block == ours

    own_halves = []
    row_at = lax.broadcasted_iota(jnp.int32, (rows, LANES), 0)
    lane_at = lax.broadcasted_iota(jnp.int32, (rows, LANES), 1)
    for i in range(rows // LANES):
        topics = tile[pl.ds(i * WIDE, 1), :]
        for j in range(1, WIDE):
            topics = jnp.where(lane_part == j, tile[pl.ds(i * WIDE + j, 1), :], topics)
        own_halves.append((topics, row_at != lane_at + i * LANES))
    against(own[...], own_halves, first=True)

    for c in beside:
        c.wait_recv()
    plane = parts[0]
    for j in range(1, WIDE):
        plane = jnp.where(lane_part == j, parts[j], plane)
    planes[0] = plane

    far = depth // 2

    def plane_at(way, hop):
        return 0 if hop == 0 else 2 * hop - 1 + way

    in_plane = {}

    def pass_plane(hop):
        for way in (0, 1):
            if hop and (way, hop) in in_plane:
                in_plane[way, hop].wait_recv()
            if hop + 1 < far or (hop + 1 == far and way == 0):
                in_plane[way, hop + 1] = copy(
                    planes.at[plane_at(way, hop)], planes.at[plane_at(way, hop + 1)],
                    dev=node(1 - 2 * way, 0))

    def finish(step):
        for c in in_slots[step]:
            c.wait_recv()
        if step == 0:
            for c in border:
                c.wait_recv()
            topics = jnp.where(lane_part == 0, edges[0, pl.ds(blocks - 1, 1), :], edges[1, pl.ds(0, 1), :])
            before = jnp.where(slab > 0, 0, -1)
            behind = jnp.where(slab < slabs - 1, blocks - 1, -1)
            ours = jnp.where(lane_part == 0, before, jnp.where(lane_part == 1, behind, -1))
            halves = [plane_half(0, 0), (topics, row_block == ours)]
        elif step == far:
            halves = [plane_half(-far, plane_at(0, far))]
        else:
            halves = [plane_half(-step, plane_at(0, step)), plane_half(step, plane_at(1, step))]
        against(groups[pl.ds(step * rows, LANES * len(halves)), :], halves)

    pass_plane(0)
    for hop in range(1, hops + 1):
        for piece in range(PIECES):
            for way in (0, 1):
                in_ring[way, hop, piece].wait_recv()
                if hop < hops:
                    in_ring[way, hop + 1, piece] = ring_step(way, hop + 1, piece)
        in_slots[hop] = []
        if hop == hops:
            in_slots[far - 1] = []
            in_slots[far] = []
            for way, offsets in ((0, (0, 1)), (1, (2, 3))):
                ring, by = rings[way * hops + hop - 1], 1 - 2 * way
                in_slots[far] += picks(ring, far, 0, -by * hop, by * 2, offsets)
                in_slots[far - 1] += picks(ring, far - 1, way, -by * hop, by, range(WIDE))
        for way in (0, 1):
            ring, by = rings[way * hops + hop - 1], 1 - 2 * way
            in_slots[hop] += picks(ring, hop, way, -by * hop, 0, range(WIDE))
        pass_plane(hop)
        finish(hop - 1)
    pass_plane(far - 1)
    finish(hops)
    pass_plane(far)
    finish(far - 1)
    finish(far)

    total = jnp.sum(weight_sum[...], axis=1, keepdims=True)
    out[...] = (acc[...] / total).astype(out.dtype)
    for c in started:
        c.wait_send()


def local(depth, slabs, embeddings, topic_ids, pair_blocks):
    rows, width = embeddings.shape
    hops = full_hops(depth)
    blocks = rows // BLOCK
    copies, picked = counts(depth)
    whole = pltpu.VMEM((rows, width), jnp.bfloat16)
    ids = pltpu.VMEM((blocks, LANES), jnp.float32)
    return pl.pallas_call(
        functools.partial(kernel, depth, slabs),
        out_shape=jax.ShapeDtypeStruct((rows, width), jnp.bfloat16),
        in_specs=[
            pl.BlockSpec(memory_space=pl.ANY),
            pl.BlockSpec(memory_space=pltpu.VMEM),
            pl.BlockSpec(memory_space=pltpu.SMEM),
        ],
        out_specs=pl.BlockSpec(memory_space=pltpu.VMEM),
        scratch_shapes=[
            whole,
            whole,
            pltpu.VMEM(((depth // 2) * rows + LANES, width), jnp.bfloat16),
            pltpu.VMEM((picked * BLOCK, width), jnp.bfloat16),
            ids,
            pltpu.VMEM((WIDE, blocks, LANES), jnp.float32),
            pltpu.VMEM((depth, blocks, LANES), jnp.float32),
            pltpu.VMEM((2, blocks, LANES), jnp.float32),
            pltpu.VMEM((rows, LANES), jnp.float32),
            pltpu.VMEM((rows, width), jnp.float32),
            pltpu.VMEM((rows, LANES), jnp.float32),
            pltpu.SemaphoreType.DMA,
            pltpu.SemaphoreType.DMA((copies,)),
            pltpu.SemaphoreType.DMA((copies,)),
        ] + [whole] * (2 * hops),
        compiler_params=pltpu.CompilerParams(
            collective_id=0, has_side_effects=True, vmem_limit_bytes=40 * 2**20),
    )(embeddings, topic_ids.reshape(1, rows), pair_blocks)


def solution(mesh):
    return jax.shard_map(
        functools.partial(local, mesh.shape["dev"] // WIDE, mesh.shape["topic"]),
        mesh=mesh,
        in_specs=(P(("topic", "dev"), None), P(("topic", "dev")), P("topic", None, None)),
        out_specs=P(("topic", "dev"), None),
        check_vma=False,
    )
```

```python
import functools

import jax
import jax.numpy as jnp
from jax import lax
from jax.experimental import pallas as pl
from jax.experimental.pallas import tpu as pltpu
from jax.sharding import PartitionSpec as P

BLOCK = 32
WIDE = 4
LANES = WIDE * BLOCK
PIECES = 2

SHARPNESS = 60.0
LEAKAGE = 0.3
EPSILON = 1e-06

MESH = pl.DeviceIdType.MESH


def full_hops(depth):
    return depth // 2 - 2


def picked_blocks(depth):
    return 3 + 2 * full_hops(depth) * 3 + 2 * 6


def kernel(depth, slabs, embed, topic, pairs, out, raw, topic_row, pair, own, groups, stage, tile, parts,
           planes, edges, mine, ours_at, theirs_at, acc, weight_sum, local_sem, send_sem, ring_sem,
           plane_sem, slot_sem, tile_sem, *rings):
    hops = full_hops(depth)
    rows, width = own.shape
    blocks = rows // BLOCK
    members = depth * WIDE
    far = depth // 2
    me = lax.axis_index("dev")
    slab = lax.axis_index("topic")
    z, x = me // WIDE, lax.rem(me, WIDE)

    def node(dz, dx):
        return lax.rem(z + dz + depth, depth) * WIDE + lax.rem(x + dx + WIDE, WIDE)

    def neighbour(by):
        return lax.rem(slab + by + slabs, slabs)

    loads = [
        pltpu.make_async_copy(src, dst, local_sem.at[i])
        for i, (src, dst) in enumerate(((embed, raw), (topic, topic_row), (pairs, pair)))
    ]
    for c in loads:
        c.start()

    barrier = pltpu.get_barrier_semaphore()
    takers = [(0, o) for o in (1, 2, 3)]
    takers += [(s, o) for s in (1, -1) for o in range(WIDE)]
    takers += [(2, 0), (2, 1), (-2, 2), (-2, 3)]
    for dz, dx in takers:
        pl.semaphore_signal(barrier, inc=1, device_id={"dev": node(-dz, -dx)}, device_id_type=MESH)
    for by in (1, -1):
        pl.semaphore_signal(barrier, inc=1, device_id={"topic": neighbour(by)}, device_id_type=MESH)

    RING, BLOCKS, EDGES, TILES = (0, 1), 2, 3, 4
    tiles_sent = [0]

    def copy(kind, arrived, src, dst, **device):
        c = pltpu.make_async_remote_copy(
            src_ref=src, dst_ref=dst, send_sem=send_sem.at[kind], recv_sem=arrived,
            device_id=device, device_id_type=MESH)
        c.start()
        if kind == TILES:
            tiles_sent[0] += 1
        return c

    def await_bytes(sem, like):
        pltpu.make_async_copy(like, like, sem).wait()

    loads[0].wait()
    values = raw[...].astype(jnp.float32)
    scale = lax.rsqrt(jnp.mean(values * values, axis=-1, keepdims=True) + EPSILON)
    own[...] = (values * scale).astype(jnp.bfloat16)

    pl.semaphore_wait(barrier, len(takers) + 2)

    def ring_step(way, hop, piece):
        src = own if hop == 1 else rings[way * hops + hop - 2]
        part = pl.ds(piece * (rows // PIECES), rows // PIECES)
        return copy(
            RING[way], ring_sem.at[way, hop - 1, piece], src.at[part],
            rings[way * hops + hop - 1].at[part], dev=node(1 - 2 * way, 0))

    in_ring = {}
    for piece in range(PIECES):
        for way in (0, 1):
            in_ring[way, 1, piece] = ring_step(way, 1, piece)

    loads[1].wait()
    ids = topic_row[...].astype(jnp.float32)
    lane_part = lax.broadcasted_iota(jnp.int32, (1, LANES), 1) // BLOCK
    of_block = lax.broadcasted_iota(jnp.int32, (blocks, rows), 0) == lax.broadcasted_iota(
        jnp.int32, (blocks, rows), 1) // BLOCK
    same_place = lax.rem(lax.broadcasted_iota(jnp.int32, (rows, LANES), 0), BLOCK) == lax.rem(
        lax.broadcasted_iota(jnp.int32, (rows, LANES), 1), BLOCK)
    tile[...] = jnp.dot(
        jnp.where(of_block, ids, 0.0).astype(jnp.bfloat16), same_place.astype(jnp.bfloat16),
        preferred_element_type=jnp.float32)
    for o in (1, 2, 3):
        copy(TILES, tile_sem, tile, parts.at[x], dev=node(0, o))
    copy(TILES, slot_sem.at[far + 1], tile, edges.at[0], topic=neighbour(1))
    copy(TILES, slot_sem.at[far + 1], tile, edges.at[1], topic=neighbour(-1))
    parts[x] = tile[...]
    copy(EDGES, slot_sem.at[0], own.at[pl.ds(rows - BLOCK, BLOCK)],
         groups.at[pl.ds(LANES, BLOCK)], topic=neighbour(1))
    copy(EDGES, slot_sem.at[0], own.at[pl.ds(0, BLOCK)],
         groups.at[pl.ds(LANES + BLOCK, BLOCK)], topic=neighbour(-1))

    def choose(owner, takers):
        count = len(takers) * BLOCK
        at = lax.broadcasted_iota(jnp.int32, (count, 1), 0)
        taker = jnp.full((count, 1), takers[0], jnp.int32)
        for i in range(1, len(takers)):
            taker = jnp.where(at >= i * BLOCK, takers[i], taker)
        named = jnp.where(
            lax.broadcasted_iota(jnp.int32, (count, members), 1) == taker,
            pair[0, pl.ds(owner, 1), :].astype(jnp.float32), 0.0)
        block = jnp.maximum(jnp.sum(named, axis=1, keepdims=True), 0.0).astype(jnp.int32)
        source = block * BLOCK + lax.rem(at, BLOCK)
        return (lax.broadcasted_iota(jnp.int32, (count, rows), 1) == source).astype(jnp.bfloat16)

    def slot(step, way):
        return groups.at[pl.ds(pl.multiple_of(step * rows + way * LANES + x * BLOCK, BLOCK), BLOCK)]

    staged = [0]

    def picks(dz_owner, dz_taker, offsets):
        takers = [node(dz_taker, o) for o in offsets]
        choice = choose(node(dz_owner, 0), takers)

        def send(src, step, way):
            picked = jnp.dot(choice, src[...], preferred_element_type=jnp.float32).astype(jnp.bfloat16)
            for i, (o, taker) in enumerate(zip(offsets, takers)):
                block = picked[i * BLOCK:(i + 1) * BLOCK]
                if dz_taker == 0 and o == 0:
                    slot(step, way)[...] = block
                    continue
                spot = stage.at[pl.ds(staged[0] * BLOCK, BLOCK)]
                staged[0] += 1
                spot[...] = block
                copy(BLOCKS, slot_sem.at[step], spot, slot(step, way), dev=taker)

        return send

    loads[2].wait()
    picks(0, 0, range(WIDE))(own, 0, 0)
    groups[pl.ds(LANES + 2 * BLOCK, 2 * BLOCK), :] = jnp.zeros((2 * BLOCK, width), jnp.bfloat16)

    ones = jnp.ones((rows, LANES), jnp.bfloat16)
    diagonal = lax.broadcasted_iota(jnp.int32, (rows, rows), 0) == lax.broadcasted_iota(
        jnp.int32, (rows, rows), 1)
    mine[...] = jnp.dot(
        jnp.where(diagonal, ids, 0.0).astype(jnp.bfloat16), ones, preferred_element_type=jnp.float32)

    in_plane_of = lax.broadcasted_iota(jnp.int32, (depth, members), 0) == lax.broadcasted_iota(
        jnp.int32, (depth, members), 1) // WIDE
    spread = lax.rem(lax.broadcasted_iota(jnp.int32, (members, LANES), 0), WIDE) == lax.broadcasted_iota(
        jnp.int32, (members, LANES), 1) // BLOCK
    my_row = pair[0, pl.ds(me, 1), :].astype(jnp.float32)
    ours_at[...] = jnp.dot(
        jnp.where(in_plane_of, my_row, 0.0).astype(jnp.bfloat16), spread.astype(jnp.bfloat16),
        preferred_element_type=jnp.float32)
    my_column = jnp.sum(
        jnp.where(lax.broadcasted_iota(jnp.int32, (members, members), 1) == me,
                  pair[0].astype(jnp.float32), 0.0), axis=1, keepdims=True)
    theirs_at[...] = jnp.dot(
        in_plane_of.astype(jnp.bfloat16), jnp.where(spread, my_column, 0.0).astype(jnp.bfloat16),
        preferred_element_type=jnp.float32)

    row_block = (lax.broadcasted_iota(jnp.int32, (rows, LANES), 0) // BLOCK).astype(jnp.float32)
    block_at = lax.broadcasted_iota(jnp.int32, (blocks, LANES), 0).astype(jnp.float32)

    def weigh(scores, topics, keep):
        factor = jnp.where(mine[...] == topics, 1.0, LEAKAGE)
        w = jnp.exp(scores * (SHARPNESS / width)) * factor
        return jnp.where(keep, w, 0.0).astype(jnp.bfloat16)

    def against(theirs, halves, first=False):
        scores = lax.dot_general(
            own[...], theirs, (((1,), (1,)), ((), ())), preferred_element_type=jnp.float32)
        ws = [
            weigh(scores[:, i * LANES:(i + 1) * LANES], topics, keep)
            for i, (topics, keep) in enumerate(halves)
        ]
        totals = sum(w.astype(jnp.float32) for w in ws)
        w = jnp.concatenate(ws, 1) if len(ws) > 1 else ws[0]
        sums = jnp.dot(w, theirs, preferred_element_type=jnp.float32)
        if first:
            acc[...] = sums
            weight_sum[...] = totals
        else:
            acc[...] += sums
            weight_sum[...] += totals

    def plane_half(dz, plane):
        at = lax.rem(z + dz + depth, depth)
        theirs, ours = theirs_at[pl.ds(at, 1), :], ours_at[pl.ds(at, 1), :]
        topics = jnp.sum(jnp.where(block_at == theirs, planes[plane], 0.0), axis=0, keepdims=True)
        return topics, row_block == ours

    own_halves = []
    row_at = lax.broadcasted_iota(jnp.int32, (rows, LANES), 0)
    lane_at = lax.broadcasted_iota(jnp.int32, (rows, LANES), 1)
    for i in range(rows // LANES):
        topics = tile[pl.ds(i * WIDE, 1), :]
        for j in range(1, WIDE):
            topics = jnp.where(lane_part == j, tile[pl.ds(i * WIDE + j, 1), :], topics)
        own_halves.append((topics, row_at != lane_at + i * LANES))
    against(own[...], own_halves, first=True)

    await_bytes(tile_sem, parts.at[pl.ds(0, WIDE - 1)])
    plane = parts[0]
    for j in range(1, WIDE):
        plane = jnp.where(lane_part == j, parts[j], plane)
    planes[0] = plane

    def plane_at(way, hop):
        return 0 if hop == 0 else 2 * hop - 1 + way

    in_plane = {}

    def pass_plane(hop):
        for way in (0, 1):
            if hop and (way, hop) in in_plane:
                in_plane[way, hop].wait_recv()
            if hop + 1 < far or (hop + 1 == far and way == 0):
                in_plane[way, hop + 1] = copy(
                    TILES, plane_sem.at[way, hop], planes.at[plane_at(way, hop)], planes.at[plane_at(way, hop + 1)],
                    dev=node(1 - 2 * way, 0))

    def finish(step):
        blocks_in = {0: WIDE - 1 + 2, far - 1: 2 * WIDE, far: WIDE}.get(step, 2 * (WIDE - 1))
        await_bytes(slot_sem.at[step], groups.at[pl.ds(step * rows, blocks_in * BLOCK)])
        if step == 0:
            await_bytes(slot_sem.at[far + 1], edges)
            topics = jnp.where(lane_part == 0, edges[0, pl.ds(blocks - 1, 1), :], edges[1, pl.ds(0, 1), :])
            before = jnp.where(slab > 0, 0.0, -1.0)
            behind = jnp.where(slab < slabs - 1, blocks - 1.0, -1.0)
            ours = jnp.where(lane_part == 0, before, jnp.where(lane_part == 1, behind, -1.0))
            halves = [plane_half(0, 0), (topics, row_block == ours)]
        elif step == far:
            halves = [plane_half(-far, plane_at(0, far))]
        else:
            halves = [plane_half(-step, plane_at(0, step)), plane_half(step, plane_at(1, step))]
        against(groups[pl.ds(step * rows, LANES * len(halves)), :], halves)

    pass_plane(0)
    for hop in range(1, hops + 1):
        sends = []
        for way, offsets in ((0, (0, 1)), (1, (2, 3))):
            ring, by = rings[way * hops + hop - 1], 1 - 2 * way
            if hop == hops:
                sends.append((picks(-by * hop, by * 2, offsets), ring, far, 0))
                sends.append((picks(-by * hop, by, range(WIDE)), ring, far - 1, way))
        for way in (0, 1):
            ring, by = rings[way * hops + hop - 1], 1 - 2 * way
            sends.append((picks(-by * hop, 0, range(WIDE)), ring, hop, way))
        for piece in range(PIECES):
            for way in (0, 1):
                in_ring[way, hop, piece].wait_recv()
                if hop < hops:
                    in_ring[way, hop + 1, piece] = ring_step(way, hop + 1, piece)
        for send, ring, step, way in sends:
            send(ring, step, way)
        pass_plane(hop)
        finish(hop - 1)
    pass_plane(far - 1)
    finish(hops)
    pass_plane(far)
    finish(far)
    finish(far - 1)

    total = jnp.sum(weight_sum[...], axis=1, keepdims=True)
    out[...] = (acc[...] / total).astype(out.dtype)
    for way in (0, 1):
        await_bytes(send_sem.at[RING[way]], groups.at[pl.ds(0, hops * rows)])
    await_bytes(send_sem.at[BLOCKS], stage)
    await_bytes(send_sem.at[EDGES], groups.at[pl.ds(0, 2 * BLOCK)])
    await_bytes(send_sem.at[TILES], mine.at[pl.ds(0, tiles_sent[0] * blocks)])


def local(depth, slabs, embeddings, topic_ids, pair_blocks):
    rows, width = embeddings.shape
    hops = full_hops(depth)
    blocks = rows // BLOCK
    far = depth // 2
    whole = pltpu.VMEM((rows, width), jnp.bfloat16)
    ids = pltpu.VMEM((blocks, LANES), jnp.float32)
    return pl.pallas_call(
        functools.partial(kernel, depth, slabs),
        out_shape=jax.ShapeDtypeStruct((rows, width), jnp.bfloat16),
        in_specs=[pl.BlockSpec(memory_space=pl.ANY)] * 3,
        out_specs=pl.BlockSpec(memory_space=pltpu.VMEM),
        scratch_shapes=[
            whole,
            pltpu.VMEM((1, rows), jnp.int32),
            pltpu.VMEM(pair_blocks.shape, jnp.int32),
            whole,
            pltpu.VMEM((far * rows + LANES, width), jnp.bfloat16),
            pltpu.VMEM((picked_blocks(depth) * BLOCK, width), jnp.bfloat16),
            ids,
            pltpu.VMEM((WIDE, blocks, LANES), jnp.float32),
            pltpu.VMEM((depth, blocks, LANES), jnp.float32),
            pltpu.VMEM((2, blocks, LANES), jnp.float32),
            pltpu.VMEM((rows, LANES), jnp.float32),
            pltpu.VMEM((depth, LANES), jnp.float32),
            pltpu.VMEM((depth, LANES), jnp.float32),
            pltpu.VMEM((rows, width), jnp.float32),
            pltpu.VMEM((rows, LANES), jnp.float32),
            pltpu.SemaphoreType.DMA((3,)),
            pltpu.SemaphoreType.DMA((5,)),
            pltpu.SemaphoreType.DMA((2, hops, PIECES)),
            pltpu.SemaphoreType.DMA((2, far)),
            pltpu.SemaphoreType.DMA((far + 2,)),
            pltpu.SemaphoreType.DMA,
        ] + [whole] * (2 * hops),
        compiler_params=pltpu.CompilerParams(
            collective_id=0, has_side_effects=True, vmem_limit_bytes=60 * 2**20),
    )(embeddings, topic_ids.reshape(1, rows), pair_blocks)


def solution(mesh):
    return jax.shard_map(
        functools.partial(local, mesh.shape["dev"] // WIDE, mesh.shape["topic"]),
        mesh=mesh,
        in_specs=(P(("topic", "dev"), None), P(("topic", "dev")), P("topic", None, None)),
        out_specs=P(("topic", "dev"), None),
        check_vma=False,
    )
```

```python
import functools

import jax
import jax.numpy as jnp
from jax import lax
from jax.experimental import pallas as pl
from jax.experimental.pallas import tpu as pltpu
from jax.sharding import PartitionSpec as P

BLOCK = 32
WIDE = 4
LANES = WIDE * BLOCK
PIECES = 2

SHARPNESS = 60.0
LEAKAGE = 0.3
EPSILON = 1e-06

MESH = pl.DeviceIdType.MESH


def full_hops(depth):
    return depth // 2 - 2


def picked_blocks(depth):
    return 3 + 2 * full_hops(depth) * 3 + 2 * 6


def kernel(depth, slabs, embed, topic, pairs, out, raw, topic_row, pair, own, groups, stage, tile, parts,
           planes, edges, mine, ours_at, theirs_at, acc, weight_sum, local_sem, send_sem, ring_sem,
           plane_sem, slot_sem, tile_sem, *rings):
    hops = full_hops(depth)
    rows, width = own.shape
    blocks = rows // BLOCK
    members = depth * WIDE
    far = depth // 2
    me = lax.axis_index("dev")
    slab = lax.axis_index("topic")
    z, x = me // WIDE, lax.rem(me, WIDE)

    def node(dz, dx):
        return lax.rem(z + dz + depth, depth) * WIDE + lax.rem(x + dx + WIDE, WIDE)

    def neighbour(by):
        return lax.rem(slab + by + slabs, slabs)

    loads = [
        pltpu.make_async_copy(src, dst, local_sem.at[i])
        for i, (src, dst) in enumerate(((embed, raw), (topic, topic_row), (pairs, pair)))
    ]
    for c in loads:
        c.start()

    barrier = pltpu.get_barrier_semaphore()
    takers = [(0, o) for o in (1, 2, 3)]
    takers += [(s, o) for s in (1, -1) for o in range(WIDE)]
    takers += [(2, 0), (2, 1), (-2, 2), (-2, 3)]
    for dz, dx in takers:
        pl.semaphore_signal(barrier, inc=1, device_id={"dev": node(-dz, -dx)}, device_id_type=MESH)
    for by in (1, -1):
        pl.semaphore_signal(barrier, inc=1, device_id={"topic": neighbour(by)}, device_id_type=MESH)

    RING, BLOCKS, EDGES, TILES = (0, 1), 2, 3, 4
    tiles_sent = [0]

    def copy(kind, arrived, src, dst, **device):
        c = pltpu.make_async_remote_copy(
            src_ref=src, dst_ref=dst, send_sem=send_sem.at[kind], recv_sem=arrived,
            device_id=device, device_id_type=MESH)
        c.start()
        if kind == TILES:
            tiles_sent[0] += 1
        return c

    def await_bytes(sem, like):
        pltpu.make_async_copy(like, like, sem).wait()

    loads[0].wait()
    values = raw[...].astype(jnp.float32)
    scale = lax.rsqrt(jnp.mean(values * values, axis=-1, keepdims=True) + EPSILON)
    own[...] = (values * scale).astype(jnp.bfloat16)

    pl.semaphore_wait(barrier, len(takers) + 2)

    def part(piece):
        return pl.ds(piece * (width // PIECES), width // PIECES)

    def ring_step(way, hop, piece):
        src = own if hop == 1 else rings[way * hops + hop - 2]
        return copy(
            RING[way], ring_sem.at[way, hop - 1, piece], src.at[:, part(piece)],
            rings[way * hops + hop - 1].at[:, part(piece)], dev=node(1 - 2 * way, 0))

    in_ring = {}
    for piece in range(PIECES):
        for way in (0, 1):
            in_ring[way, 1, piece] = ring_step(way, 1, piece)

    loads[1].wait()
    ids = topic_row[...].astype(jnp.float32)
    lane_part = lax.broadcasted_iota(jnp.int32, (1, LANES), 1) // BLOCK
    of_block = lax.broadcasted_iota(jnp.int32, (blocks, rows), 0) == lax.broadcasted_iota(
        jnp.int32, (blocks, rows), 1) // BLOCK
    same_place = lax.rem(lax.broadcasted_iota(jnp.int32, (rows, LANES), 0), BLOCK) == lax.rem(
        lax.broadcasted_iota(jnp.int32, (rows, LANES), 1), BLOCK)
    tile[...] = jnp.dot(
        jnp.where(of_block, ids, 0.0).astype(jnp.bfloat16), same_place.astype(jnp.bfloat16),
        preferred_element_type=jnp.float32)
    for o in (1, 2, 3):
        copy(TILES, tile_sem, tile, parts.at[x], dev=node(0, o))
    copy(TILES, slot_sem.at[far + 1], tile, edges.at[0], topic=neighbour(1))
    copy(TILES, slot_sem.at[far + 1], tile, edges.at[1], topic=neighbour(-1))
    parts[x] = tile[...]
    copy(EDGES, slot_sem.at[0], own.at[pl.ds(rows - BLOCK, BLOCK)],
         groups.at[pl.ds(LANES, BLOCK)], topic=neighbour(1))
    copy(EDGES, slot_sem.at[0], own.at[pl.ds(0, BLOCK)],
         groups.at[pl.ds(LANES + BLOCK, BLOCK)], topic=neighbour(-1))

    def choose(owner, takers):
        count = len(takers) * BLOCK
        at = lax.broadcasted_iota(jnp.int32, (count, 1), 0)
        taker = jnp.full((count, 1), takers[0], jnp.int32)
        for i in range(1, len(takers)):
            taker = jnp.where(at >= i * BLOCK, takers[i], taker)
        named = jnp.where(
            lax.broadcasted_iota(jnp.int32, (count, members), 1) == taker,
            pair[0, pl.ds(owner, 1), :].astype(jnp.float32), 0.0)
        block = jnp.maximum(jnp.sum(named, axis=1, keepdims=True), 0.0).astype(jnp.int32)
        source = block * BLOCK + lax.rem(at, BLOCK)
        return (lax.broadcasted_iota(jnp.int32, (count, rows), 1) == source).astype(jnp.bfloat16)

    def slot(step, way):
        return groups.at[pl.ds(pl.multiple_of(step * rows + way * LANES + x * BLOCK, BLOCK), BLOCK)]

    staged = [0]

    def picks(dz_owner, dz_taker, offsets):
        takers = [node(dz_taker, o) for o in offsets]
        choice = choose(node(dz_owner, 0), takers)

        spots = []
        for o in offsets:
            local = dz_taker == 0 and o == 0
            spots.append(None if local else stage.at[pl.ds(staged[0] * BLOCK, BLOCK)])
            staged[0] += not local

        def send(src, step, way, piece):
            picked = jnp.dot(
                choice, src[:, part(piece)], preferred_element_type=jnp.float32).astype(jnp.bfloat16)
            for i, (taker, spot) in enumerate(zip(takers, spots)):
                block = picked[i * BLOCK:(i + 1) * BLOCK]
                there = slot(step, way).at[:, part(piece)]
                if spot is None:
                    there[...] = block
                    continue
                here = spot.at[:, part(piece)]
                here[...] = block
                copy(BLOCKS, slot_sem.at[step], here, there, dev=taker)

        return send

    loads[2].wait()
    pick_own = picks(0, 0, range(WIDE))
    for piece in range(PIECES):
        pick_own(own, 0, 0, piece)
    groups[pl.ds(LANES + 2 * BLOCK, 2 * BLOCK), :] = jnp.zeros((2 * BLOCK, width), jnp.bfloat16)

    ones = jnp.ones((rows, LANES), jnp.bfloat16)
    diagonal = lax.broadcasted_iota(jnp.int32, (rows, rows), 0) == lax.broadcasted_iota(
        jnp.int32, (rows, rows), 1)
    mine[...] = jnp.dot(
        jnp.where(diagonal, ids, 0.0).astype(jnp.bfloat16), ones, preferred_element_type=jnp.float32)

    in_plane_of = lax.broadcasted_iota(jnp.int32, (depth, members), 0) == lax.broadcasted_iota(
        jnp.int32, (depth, members), 1) // WIDE
    spread = lax.rem(lax.broadcasted_iota(jnp.int32, (members, LANES), 0), WIDE) == lax.broadcasted_iota(
        jnp.int32, (members, LANES), 1) // BLOCK
    my_row = pair[0, pl.ds(me, 1), :].astype(jnp.float32)
    ours_at[...] = jnp.dot(
        jnp.where(in_plane_of, my_row, 0.0).astype(jnp.bfloat16), spread.astype(jnp.bfloat16),
        preferred_element_type=jnp.float32)
    my_column = jnp.sum(
        jnp.where(lax.broadcasted_iota(jnp.int32, (members, members), 1) == me,
                  pair[0].astype(jnp.float32), 0.0), axis=1, keepdims=True)
    theirs_at[...] = jnp.dot(
        in_plane_of.astype(jnp.bfloat16), jnp.where(spread, my_column, 0.0).astype(jnp.bfloat16),
        preferred_element_type=jnp.float32)

    row_block = (lax.broadcasted_iota(jnp.int32, (rows, LANES), 0) // BLOCK).astype(jnp.float32)
    block_at = lax.broadcasted_iota(jnp.int32, (blocks, LANES), 0).astype(jnp.float32)

    def weigh(scores, topics, keep):
        factor = jnp.where(mine[...] == topics, 1.0, LEAKAGE)
        w = jnp.exp(scores * (SHARPNESS / width)) * factor
        return jnp.where(keep, w, 0.0).astype(jnp.bfloat16)

    def against(theirs, halves, first=False):
        scores = lax.dot_general(
            own[...], theirs, (((1,), (1,)), ((), ())), preferred_element_type=jnp.float32)
        ws = [
            weigh(scores[:, i * LANES:(i + 1) * LANES], topics, keep)
            for i, (topics, keep) in enumerate(halves)
        ]
        totals = sum(w.astype(jnp.float32) for w in ws)
        w = jnp.concatenate(ws, 1) if len(ws) > 1 else ws[0]
        sums = jnp.dot(w, theirs, preferred_element_type=jnp.float32)
        if first:
            acc[...] = sums
            weight_sum[...] = totals
        else:
            acc[...] += sums
            weight_sum[...] += totals

    def plane_half(dz, plane):
        at = lax.rem(z + dz + depth, depth)
        theirs, ours = theirs_at[pl.ds(at, 1), :], ours_at[pl.ds(at, 1), :]
        topics = jnp.sum(jnp.where(block_at == theirs, planes[plane], 0.0), axis=0, keepdims=True)
        return topics, row_block == ours

    own_halves = []
    row_at = lax.broadcasted_iota(jnp.int32, (rows, LANES), 0)
    lane_at = lax.broadcasted_iota(jnp.int32, (rows, LANES), 1)
    for i in range(rows // LANES):
        topics = tile[pl.ds(i * WIDE, 1), :]
        for j in range(1, WIDE):
            topics = jnp.where(lane_part == j, tile[pl.ds(i * WIDE + j, 1), :], topics)
        own_halves.append((topics, row_at != lane_at + i * LANES))
    against(own[...], own_halves, first=True)

    await_bytes(tile_sem, parts.at[pl.ds(0, WIDE - 1)])
    plane = parts[0]
    for j in range(1, WIDE):
        plane = jnp.where(lane_part == j, parts[j], plane)
    planes[0] = plane

    def plane_at(way, hop):
        return 0 if hop == 0 else 2 * hop - 1 + way

    in_plane = {}

    def pass_plane(hop):
        for way in (0, 1):
            if hop and (way, hop) in in_plane:
                in_plane[way, hop].wait_recv()
            if hop + 1 < far or (hop + 1 == far and way == 0):
                in_plane[way, hop + 1] = copy(
                    TILES, plane_sem.at[way, hop], planes.at[plane_at(way, hop)], planes.at[plane_at(way, hop + 1)],
                    dev=node(1 - 2 * way, 0))

    def finish(step):
        blocks_in = {0: WIDE - 1 + 2, far - 1: 2 * WIDE, far: WIDE}.get(step, 2 * (WIDE - 1))
        await_bytes(slot_sem.at[step], groups.at[pl.ds(step * rows, blocks_in * BLOCK)])
        if step == 0:
            await_bytes(slot_sem.at[far + 1], edges)
            topics = jnp.where(lane_part == 0, edges[0, pl.ds(blocks - 1, 1), :], edges[1, pl.ds(0, 1), :])
            before = jnp.where(slab > 0, 0.0, -1.0)
            behind = jnp.where(slab < slabs - 1, blocks - 1.0, -1.0)
            ours = jnp.where(lane_part == 0, before, jnp.where(lane_part == 1, behind, -1.0))
            halves = [plane_half(0, 0), (topics, row_block == ours)]
        elif step == far:
            halves = [plane_half(-far, plane_at(0, far))]
        else:
            halves = [plane_half(-step, plane_at(0, step)), plane_half(step, plane_at(1, step))]
        against(groups[pl.ds(step * rows, LANES * len(halves)), :], halves)

    pass_plane(0)
    for hop in range(1, hops + 1):
        sends = []
        for way, offsets in ((0, (0, 1)), (1, (2, 3))):
            ring, by = rings[way * hops + hop - 1], 1 - 2 * way
            if hop == hops:
                sends.append((picks(-by * hop, by * 2, offsets), ring, far, 0))
                sends.append((picks(-by * hop, by, range(WIDE)), ring, far - 1, way))
        for way in (0, 1):
            ring, by = rings[way * hops + hop - 1], 1 - 2 * way
            sends.append((picks(-by * hop, 0, range(WIDE)), ring, hop, way))
        for piece in range(PIECES):
            for way in (0, 1):
                in_ring[way, hop, piece].wait_recv()
                if hop < hops:
                    in_ring[way, hop + 1, piece] = ring_step(way, hop + 1, piece)
            for send, ring, step, way in sends:
                send(ring, step, way, piece)
        pass_plane(hop)
        finish(hop - 1)
    pass_plane(far - 1)
    finish(hops)
    pass_plane(far)
    finish(far)
    finish(far - 1)

    total = jnp.sum(weight_sum[...], axis=1, keepdims=True)
    out[...] = (acc[...] / total).astype(out.dtype)
    for way in (0, 1):
        await_bytes(send_sem.at[RING[way]], groups.at[pl.ds(0, hops * rows)])
    await_bytes(send_sem.at[BLOCKS], stage)
    await_bytes(send_sem.at[EDGES], groups.at[pl.ds(0, 2 * BLOCK)])
    await_bytes(send_sem.at[TILES], mine.at[pl.ds(0, tiles_sent[0] * blocks)])


def local(depth, slabs, embeddings, topic_ids, pair_blocks):
    rows, width = embeddings.shape
    hops = full_hops(depth)
    blocks = rows // BLOCK
    far = depth // 2
    whole = pltpu.VMEM((rows, width), jnp.bfloat16)
    ids = pltpu.VMEM((blocks, LANES), jnp.float32)
    return pl.pallas_call(
        functools.partial(kernel, depth, slabs),
        out_shape=pltpu.VMEM((rows, width), jnp.bfloat16),
        in_specs=[pl.BlockSpec(memory_space=pl.ANY)] * 3,
        out_specs=pl.BlockSpec(memory_space=pltpu.VMEM),
        scratch_shapes=[
            whole,
            pltpu.VMEM((1, rows), jnp.int32),
            pltpu.VMEM(pair_blocks.shape, jnp.int32),
            whole,
            pltpu.VMEM((far * rows + LANES, width), jnp.bfloat16),
            pltpu.VMEM((picked_blocks(depth) * BLOCK, width), jnp.bfloat16),
            ids,
            pltpu.VMEM((WIDE, blocks, LANES), jnp.float32),
            pltpu.VMEM((depth, blocks, LANES), jnp.float32),
            pltpu.VMEM((2, blocks, LANES), jnp.float32),
            pltpu.VMEM((rows, LANES), jnp.float32),
            pltpu.VMEM((depth, LANES), jnp.float32),
            pltpu.VMEM((depth, LANES), jnp.float32),
            pltpu.VMEM((rows, width), jnp.float32),
            pltpu.VMEM((rows, LANES), jnp.float32),
            pltpu.SemaphoreType.DMA((3,)),
            pltpu.SemaphoreType.DMA((5,)),
            pltpu.SemaphoreType.DMA((2, hops, PIECES)),
            pltpu.SemaphoreType.DMA((2, far)),
            pltpu.SemaphoreType.DMA((far + 2,)),
            pltpu.SemaphoreType.DMA,
        ] + [whole] * (2 * hops),
        compiler_params=pltpu.CompilerParams(
            collective_id=0, has_side_effects=True, vmem_limit_bytes=60 * 2**20),
    )(embeddings, topic_ids.reshape(1, rows), pair_blocks)


def solution(mesh):
    return jax.shard_map(
        functools.partial(local, mesh.shape["dev"] // WIDE, mesh.shape["topic"]),
        mesh=mesh,
        in_specs=(P(("topic", "dev"), None), P(("topic", "dev")), P("topic", None, None)),
        out_specs=P(("topic", "dev"), None),
        check_vma=False,
    )
```

```python
import functools

import jax
import jax.numpy as jnp
from jax import lax
from jax.experimental import pallas as pl
from jax.experimental.pallas import tpu as pltpu
from jax.sharding import PartitionSpec as P

BLOCK = 32
WIDE = 4
LANES = WIDE * BLOCK
PIECES = 3

SHARPNESS = 60.0
LEAKAGE = 0.3
EPSILON = 1e-06

MESH = pl.DeviceIdType.MESH


def full_hops(depth):
    return depth // 2 - 2


def picked_blocks(depth):
    return 3 + 2 * full_hops(depth) * 3 + 2 * 6


def kernel(depth, slabs, embed, topic, pairs, out, raw, topic_row, pair, own, groups, stage, tile, parts,
           planes, edges, mine, ours_at, theirs_at, acc, weight_sum, local_sem, send_sem, ring_sem,
           plane_sem, slot_sem, tile_sem, *rings):
    hops = full_hops(depth)
    rows, width = own.shape
    blocks = rows // BLOCK
    members = depth * WIDE
    far = depth // 2
    me = lax.axis_index("dev")
    slab = lax.axis_index("topic")
    z, x = me // WIDE, lax.rem(me, WIDE)

    def node(dz, dx):
        return lax.rem(z + dz + depth, depth) * WIDE + lax.rem(x + dx + WIDE, WIDE)

    def neighbour(by):
        return lax.rem(slab + by + slabs, slabs)

    loads = [
        pltpu.make_async_copy(src, dst, local_sem.at[i])
        for i, (src, dst) in enumerate(((embed, raw), (topic, topic_row), (pairs, pair)))
    ]
    for c in loads:
        c.start()

    barrier = pltpu.get_barrier_semaphore()
    takers = [(0, o) for o in (1, 2, 3)]
    takers += [(s, o) for s in (1, -1) for o in range(WIDE)]
    takers += [(2, 0), (2, 1), (-2, 2), (-2, 3)]
    for dz, dx in takers:
        pl.semaphore_signal(barrier, inc=1, device_id={"dev": node(-dz, -dx)}, device_id_type=MESH)
    for by in (1, -1):
        pl.semaphore_signal(barrier, inc=1, device_id={"topic": neighbour(by)}, device_id_type=MESH)

    RING, BLOCKS, EDGES, TILES = (0, 1), 2, 3, 4
    tiles_sent = [0]

    def copy(kind, arrived, src, dst, **device):
        c = pltpu.make_async_remote_copy(
            src_ref=src, dst_ref=dst, send_sem=send_sem.at[kind], recv_sem=arrived,
            device_id=device, device_id_type=MESH)
        c.start()
        if kind == TILES:
            tiles_sent[0] += 1
        return c

    def await_bytes(sem, like):
        pltpu.make_async_copy(like, like, sem).wait()

    loads[0].wait()
    values = raw[...].astype(jnp.float32)
    scale = lax.rsqrt(jnp.mean(values * values, axis=-1, keepdims=True) + EPSILON)
    own[...] = (values * scale).astype(jnp.bfloat16)

    pl.semaphore_wait(barrier, len(takers) + 2)

    def part(piece):
        return pl.ds(piece * (width // PIECES), width // PIECES)

    def ring_step(way, hop, piece):
        src = own if hop == 1 else rings[way * hops + hop - 2]
        return copy(
            RING[way], ring_sem.at[way, hop - 1, piece], src.at[:, part(piece)],
            rings[way * hops + hop - 1].at[:, part(piece)], dev=node(1 - 2 * way, 0))

    in_ring = {}
    for piece in range(PIECES):
        for way in (0, 1):
            in_ring[way, 1, piece] = ring_step(way, 1, piece)

    loads[1].wait()
    ids = topic_row[...].astype(jnp.float32)
    lane_part = lax.broadcasted_iota(jnp.int32, (1, LANES), 1) // BLOCK
    of_block = lax.broadcasted_iota(jnp.int32, (blocks, rows), 0) == lax.broadcasted_iota(
        jnp.int32, (blocks, rows), 1) // BLOCK
    same_place = lax.rem(lax.broadcasted_iota(jnp.int32, (rows, LANES), 0), BLOCK) == lax.rem(
        lax.broadcasted_iota(jnp.int32, (rows, LANES), 1), BLOCK)
    tile[...] = jnp.dot(
        jnp.where(of_block, ids, 0.0).astype(jnp.bfloat16), same_place.astype(jnp.bfloat16),
        preferred_element_type=jnp.float32)
    for o in (1, 2, 3):
        copy(TILES, tile_sem, tile, parts.at[x], dev=node(0, o))
    copy(TILES, slot_sem.at[far + 1], tile, edges.at[0], topic=neighbour(1))
    copy(TILES, slot_sem.at[far + 1], tile, edges.at[1], topic=neighbour(-1))
    parts[x] = tile[...]
    copy(EDGES, slot_sem.at[0], own.at[pl.ds(rows - BLOCK, BLOCK)],
         groups.at[pl.ds(LANES, BLOCK)], topic=neighbour(1))
    copy(EDGES, slot_sem.at[0], own.at[pl.ds(0, BLOCK)],
         groups.at[pl.ds(LANES + BLOCK, BLOCK)], topic=neighbour(-1))

    def choose(owner, takers):
        count = len(takers) * BLOCK
        at = lax.broadcasted_iota(jnp.int32, (count, 1), 0)
        taker = jnp.full((count, 1), takers[0], jnp.int32)
        for i in range(1, len(takers)):
            taker = jnp.where(at >= i * BLOCK, takers[i], taker)
        named = jnp.where(
            lax.broadcasted_iota(jnp.int32, (count, members), 1) == taker,
            pair[0, pl.ds(owner, 1), :].astype(jnp.float32), 0.0)
        block = jnp.maximum(jnp.sum(named, axis=1, keepdims=True), 0.0).astype(jnp.int32)
        source = block * BLOCK + lax.rem(at, BLOCK)
        return (lax.broadcasted_iota(jnp.int32, (count, rows), 1) == source).astype(jnp.bfloat16)

    def slot(step, way):
        return groups.at[pl.ds(pl.multiple_of(step * rows + way * LANES + x * BLOCK, BLOCK), BLOCK)]

    staged = [0]

    def picks(dz_owner, dz_taker, offsets):
        takers = [node(dz_taker, o) for o in offsets]
        choice = choose(node(dz_owner, 0), takers)

        spots = []
        for o in offsets:
            local = dz_taker == 0 and o == 0
            spots.append(None if local else stage.at[pl.ds(staged[0] * BLOCK, BLOCK)])
            staged[0] += not local

        def send(src, step, way, piece):
            picked = jnp.dot(
                choice, src[:, part(piece)], preferred_element_type=jnp.float32).astype(jnp.bfloat16)
            for i, (taker, spot) in enumerate(zip(takers, spots)):
                block = picked[i * BLOCK:(i + 1) * BLOCK]
                there = slot(step, way).at[:, part(piece)]
                if spot is None:
                    there[...] = block
                    continue
                here = spot.at[:, part(piece)]
                here[...] = block
                copy(BLOCKS, slot_sem.at[step], here, there, dev=taker)

        return send

    loads[2].wait()
    pick_own = picks(0, 0, range(WIDE))
    for piece in range(PIECES):
        pick_own(own, 0, 0, piece)
    groups[pl.ds(LANES + 2 * BLOCK, 2 * BLOCK), :] = jnp.zeros((2 * BLOCK, width), jnp.bfloat16)

    ones = jnp.ones((rows, LANES), jnp.bfloat16)
    diagonal = lax.broadcasted_iota(jnp.int32, (rows, rows), 0) == lax.broadcasted_iota(
        jnp.int32, (rows, rows), 1)
    mine[...] = jnp.dot(
        jnp.where(diagonal, ids, 0.0).astype(jnp.bfloat16), ones, preferred_element_type=jnp.float32)

    in_plane_of = lax.broadcasted_iota(jnp.int32, (depth, members), 0) == lax.broadcasted_iota(
        jnp.int32, (depth, members), 1) // WIDE
    spread = lax.rem(lax.broadcasted_iota(jnp.int32, (members, LANES), 0), WIDE) == lax.broadcasted_iota(
        jnp.int32, (members, LANES), 1) // BLOCK
    my_row = pair[0, pl.ds(me, 1), :].astype(jnp.float32)
    ours_at[...] = jnp.dot(
        jnp.where(in_plane_of, my_row, 0.0).astype(jnp.bfloat16), spread.astype(jnp.bfloat16),
        preferred_element_type=jnp.float32)
    my_column = jnp.sum(
        jnp.where(lax.broadcasted_iota(jnp.int32, (members, members), 1) == me,
                  pair[0].astype(jnp.float32), 0.0), axis=1, keepdims=True)
    theirs_at[...] = jnp.dot(
        in_plane_of.astype(jnp.bfloat16), jnp.where(spread, my_column, 0.0).astype(jnp.bfloat16),
        preferred_element_type=jnp.float32)

    row_block = (lax.broadcasted_iota(jnp.int32, (rows, LANES), 0) // BLOCK).astype(jnp.float32)
    block_at = lax.broadcasted_iota(jnp.int32, (blocks, LANES), 0).astype(jnp.float32)

    def weigh(scores, topics, keep):
        factor = jnp.where(mine[...] == topics, 1.0, LEAKAGE)
        w = jnp.exp(scores * (SHARPNESS / width)) * factor
        return jnp.where(keep, w, 0.0).astype(jnp.bfloat16)

    def against(theirs, halves, first=False, last=False):
        scores = lax.dot_general(
            own[...], theirs, (((1,), (1,)), ((), ())), preferred_element_type=jnp.float32)
        ws = [
            weigh(scores[:, i * LANES:(i + 1) * LANES], topics, keep)
            for i, (topics, keep) in enumerate(halves)
        ]
        totals = sum(w.astype(jnp.float32) for w in ws)
        w = jnp.concatenate(ws, 1) if len(ws) > 1 else ws[0]
        sums = jnp.dot(w, theirs, preferred_element_type=jnp.float32)
        if first:
            acc[...] = sums
            weight_sum[...] = totals
        elif last:
            scale = 1.0 / jnp.sum(weight_sum[...] + totals, axis=1, keepdims=True)
            out[...] = ((acc[...] + sums) * scale).astype(out.dtype)
        else:
            acc[...] += sums
            weight_sum[...] += totals

    def plane_half(dz, plane):
        at = lax.rem(z + dz + depth, depth)
        theirs, ours = theirs_at[pl.ds(at, 1), :], ours_at[pl.ds(at, 1), :]
        topics = jnp.sum(jnp.where(block_at == theirs, planes[plane], 0.0), axis=0, keepdims=True)
        return topics, row_block == ours

    own_halves = []
    row_at = lax.broadcasted_iota(jnp.int32, (rows, LANES), 0)
    lane_at = lax.broadcasted_iota(jnp.int32, (rows, LANES), 1)
    for i in range(rows // LANES):
        topics = tile[pl.ds(i * WIDE, 1), :]
        for j in range(1, WIDE):
            topics = jnp.where(lane_part == j, tile[pl.ds(i * WIDE + j, 1), :], topics)
        own_halves.append((topics, row_at != lane_at + i * LANES))
    against(own[...], own_halves, first=True)

    await_bytes(tile_sem, parts.at[pl.ds(0, WIDE - 1)])
    plane = parts[0]
    for j in range(1, WIDE):
        plane = jnp.where(lane_part == j, parts[j], plane)
    planes[0] = plane

    def plane_at(way, hop):
        return 0 if hop == 0 else 2 * hop - 1 + way

    in_plane = {}

    def pass_plane(hop):
        for way in (0, 1):
            if hop:
                in_plane[way, hop].wait_recv()
            for further in (1, 2) if hop == hops and way == 0 else (1,):
                in_plane[way, hop + further] = copy(
                    TILES, plane_sem.at[way, hop + further - 1], planes.at[plane_at(way, hop)],
                    planes.at[plane_at(way, hop + further)], dev=node(further * (1 - 2 * way), 0))

    def finish(step):
        blocks_in = {0: WIDE - 1 + 2, far - 1: 2 * WIDE, far: WIDE}.get(step, 2 * (WIDE - 1))
        await_bytes(slot_sem.at[step], groups.at[pl.ds(step * rows, blocks_in * BLOCK)])
        if step == 0:
            await_bytes(slot_sem.at[far + 1], edges)
            topics = jnp.where(lane_part == 0, edges[0, pl.ds(blocks - 1, 1), :], edges[1, pl.ds(0, 1), :])
            before = jnp.where(slab > 0, 0.0, -1.0)
            behind = jnp.where(slab < slabs - 1, blocks - 1.0, -1.0)
            ours = jnp.where(lane_part == 0, before, jnp.where(lane_part == 1, behind, -1.0))
            halves = [plane_half(0, 0), (topics, row_block == ours)]
        elif step == far:
            in_plane[0, far].wait_recv()
            halves = [plane_half(-far, plane_at(0, far))]
        else:
            if step == far - 1:
                for way in (0, 1):
                    in_plane[way, step].wait_recv()
            halves = [plane_half(-step, plane_at(0, step)), plane_half(step, plane_at(1, step))]
        against(groups[pl.ds(step * rows, LANES * len(halves)), :], halves, last=step == far - 1)

    pass_plane(0)
    for hop in range(1, hops + 1):
        sends = []
        for way, offsets in ((0, (0, 1)), (1, (2, 3))):
            ring, by = rings[way * hops + hop - 1], 1 - 2 * way
            if hop == hops:
                sends.append((picks(-by * hop, by * 2, offsets), ring, far, 0))
                sends.append((picks(-by * hop, by, range(WIDE)), ring, far - 1, way))
        for way in (0, 1):
            ring, by = rings[way * hops + hop - 1], 1 - 2 * way
            sends.append((picks(-by * hop, 0, range(WIDE)), ring, hop, way))
        for piece in range(PIECES):
            if hop == 1 and piece == 1:
                pass_plane(hop)
            for way in (0, 1):
                in_ring[way, hop, piece].wait_recv()
                if hop < hops:
                    in_ring[way, hop + 1, piece] = ring_step(way, hop + 1, piece)
            if hop > 1 and piece == 0:
                pass_plane(hop)
            for send, ring, step, way in sends:
                send(ring, step, way, piece)
        finish(hop - 1)
    finish(hops)
    finish(far)
    finish(far - 1)

    for way in (0, 1):
        await_bytes(send_sem.at[RING[way]], groups.at[pl.ds(0, hops * rows)])
    await_bytes(send_sem.at[BLOCKS], stage)
    await_bytes(send_sem.at[EDGES], groups.at[pl.ds(0, 2 * BLOCK)])
    await_bytes(send_sem.at[TILES], mine.at[pl.ds(0, tiles_sent[0] * blocks)])


def local(depth, slabs, embeddings, topic_ids, pair_blocks):
    rows, width = embeddings.shape
    hops = full_hops(depth)
    blocks = rows // BLOCK
    far = depth // 2
    whole = pltpu.VMEM((rows, width), jnp.bfloat16)
    ids = pltpu.VMEM((blocks, LANES), jnp.float32)
    return pl.pallas_call(
        functools.partial(kernel, depth, slabs),
        out_shape=pltpu.VMEM((rows, width), jnp.bfloat16),
        in_specs=[pl.BlockSpec(memory_space=pl.ANY)] * 3,
        out_specs=pl.BlockSpec(memory_space=pltpu.VMEM),
        scratch_shapes=[
            whole,
            pltpu.VMEM((1, rows), jnp.int32),
            pltpu.VMEM(pair_blocks.shape, jnp.int32),
            whole,
            pltpu.VMEM((far * rows + LANES, width), jnp.bfloat16),
            pltpu.VMEM((picked_blocks(depth) * BLOCK, width), jnp.bfloat16),
            ids,
            pltpu.VMEM((WIDE, blocks, LANES), jnp.float32),
            pltpu.VMEM((depth, blocks, LANES), jnp.float32),
            pltpu.VMEM((2, blocks, LANES), jnp.float32),
            pltpu.VMEM((rows, LANES), jnp.float32),
            pltpu.VMEM((depth, LANES), jnp.float32),
            pltpu.VMEM((depth, LANES), jnp.float32),
            pltpu.VMEM((rows, width), jnp.float32),
            pltpu.VMEM((rows, LANES), jnp.float32),
            pltpu.SemaphoreType.DMA((3,)),
            pltpu.SemaphoreType.DMA((5,)),
            pltpu.SemaphoreType.DMA((2, hops, PIECES)),
            pltpu.SemaphoreType.DMA((2, far)),
            pltpu.SemaphoreType.DMA((far + 2,)),
            pltpu.SemaphoreType.DMA,
        ] + [whole] * (2 * hops),
        compiler_params=pltpu.CompilerParams(
            collective_id=0, has_side_effects=True, vmem_limit_bytes=60 * 2**20),
    )(embeddings, topic_ids.reshape(1, rows), pair_blocks)


def solution(mesh):
    return jax.shard_map(
        functools.partial(local, mesh.shape["dev"] // WIDE, mesh.shape["topic"]),
        mesh=mesh,
        in_specs=(P(("topic", "dev"), None), P(("topic", "dev")), P("topic", None, None)),
        out_specs=P(("topic", "dev"), None),
        check_vma=False,
    )
```

```python
import functools

import jax
import jax.numpy as jnp
from jax import lax
from jax.experimental import pallas as pl
from jax.experimental.pallas import tpu as pltpu
from jax.sharding import PartitionSpec as P

BLOCK = 32
WIDE = 4
LANES = WIDE * BLOCK
PIECES = 3

SHARPNESS = 60.0
LEAKAGE = 0.3
EPSILON = 1e-06

MESH = pl.DeviceIdType.MESH


def full_hops(depth):
    return depth // 2 - 2


def picked_blocks(depth):
    return 3 + 2 * full_hops(depth) * 3 + 2 * 6


def kernel(depth, slabs, embed, topic, pairs, out, raw, topic_row, pair, own, groups, stage, tile, parts,
           planes, edges, mine, ours_at, theirs_at, acc, weight_sum, local_sem, send_sem, ring_sem,
           plane_sem, slot_sem, tile_sem, *rings):
    hops = full_hops(depth)
    rows, width = own.shape
    blocks = rows // BLOCK
    members = depth * WIDE
    far = depth // 2
    me = lax.axis_index("dev")
    slab = lax.axis_index("topic")
    z, x = me // WIDE, lax.rem(me, WIDE)

    def node(dz, dx):
        return lax.rem(z + dz + depth, depth) * WIDE + lax.rem(x + dx + WIDE, WIDE)

    def neighbour(by):
        return lax.rem(slab + by + slabs, slabs)

    loads = [
        pltpu.make_async_copy(src, dst, local_sem.at[i])
        for i, (src, dst) in enumerate(((embed, raw), (topic, topic_row), (pairs, pair)))
    ]
    for c in loads:
        c.start()

    barrier = pltpu.get_barrier_semaphore()
    takers = [(0, o) for o in (1, 2, 3)]
    takers += [(s, o) for s in (1, -1) for o in range(WIDE)]
    takers += [(2, 0), (2, 1), (-2, 2), (-2, 3)]
    for dz, dx in takers:
        pl.semaphore_signal(barrier, inc=1, device_id={"dev": node(-dz, -dx)}, device_id_type=MESH)
    for by in (1, -1):
        pl.semaphore_signal(barrier, inc=1, device_id={"topic": neighbour(by)}, device_id_type=MESH)

    RING, BLOCKS, EDGES, TILES = (0, 1), 2, 3, 4
    tiles_sent = [0]

    def copy(kind, arrived, src, dst, **device):
        c = pltpu.make_async_remote_copy(
            src_ref=src, dst_ref=dst, send_sem=send_sem.at[kind], recv_sem=arrived,
            device_id=device, device_id_type=MESH)
        c.start()
        if kind == TILES:
            tiles_sent[0] += 1
        return c

    def await_bytes(sem, like):
        pltpu.make_async_copy(like, like, sem).wait()

    loads[0].wait()
    values = raw[...].astype(jnp.float32)
    scale = lax.rsqrt(jnp.mean(values * values, axis=-1, keepdims=True) + EPSILON)
    own[...] = (values * scale).astype(jnp.bfloat16)

    pl.semaphore_wait(barrier, len(takers) + 2)

    def part(piece):
        if piece is None:
            return pl.ds(0, width)
        return pl.ds(piece * (width // PIECES), width // PIECES)

    def ring_step(way, hop, piece):
        src = own if hop == 1 else rings[way * hops + hop - 2]
        return copy(
            RING[way], ring_sem.at[way, hop - 1, piece], src.at[:, part(piece)],
            rings[way * hops + hop - 1].at[:, part(piece)], dev=node(1 - 2 * way, 0))

    in_ring = {}
    for piece in range(PIECES):
        for way in (0, 1):
            in_ring[way, 1, piece] = ring_step(way, 1, piece)

    loads[1].wait()
    ids = topic_row[...].astype(jnp.float32)
    lane_part = lax.broadcasted_iota(jnp.int32, (1, LANES), 1) // BLOCK
    of_block = lax.broadcasted_iota(jnp.int32, (blocks, rows), 0) == lax.broadcasted_iota(
        jnp.int32, (blocks, rows), 1) // BLOCK
    same_place = lax.rem(lax.broadcasted_iota(jnp.int32, (rows, LANES), 0), BLOCK) == lax.rem(
        lax.broadcasted_iota(jnp.int32, (rows, LANES), 1), BLOCK)
    tile[...] = jnp.dot(
        jnp.where(of_block, ids, 0.0).astype(jnp.bfloat16), same_place.astype(jnp.bfloat16),
        preferred_element_type=jnp.float32)
    for o in (1, 2, 3):
        copy(TILES, tile_sem, tile, parts.at[x], dev=node(0, o))
    copy(TILES, slot_sem.at[far + 1], tile, edges.at[0], topic=neighbour(1))
    copy(TILES, slot_sem.at[far + 1], tile, edges.at[1], topic=neighbour(-1))
    parts[x] = tile[...]
    copy(EDGES, slot_sem.at[0], own.at[pl.ds(rows - BLOCK, BLOCK)],
         groups.at[pl.ds(LANES, BLOCK)], topic=neighbour(1))
    copy(EDGES, slot_sem.at[0], own.at[pl.ds(0, BLOCK)],
         groups.at[pl.ds(LANES + BLOCK, BLOCK)], topic=neighbour(-1))

    def choose(owner, takers):
        count = len(takers) * BLOCK
        at = lax.broadcasted_iota(jnp.int32, (count, 1), 0)
        taker = jnp.full((count, 1), takers[0], jnp.int32)
        for i in range(1, len(takers)):
            taker = jnp.where(at >= i * BLOCK, takers[i], taker)
        named = jnp.where(
            lax.broadcasted_iota(jnp.int32, (count, members), 1) == taker,
            pair[0, pl.ds(owner, 1), :].astype(jnp.float32), 0.0)
        block = jnp.maximum(jnp.sum(named, axis=1, keepdims=True), 0.0).astype(jnp.int32)
        source = block * BLOCK + lax.rem(at, BLOCK)
        return (lax.broadcasted_iota(jnp.int32, (count, rows), 1) == source).astype(jnp.bfloat16)

    def slot(step, way):
        return groups.at[pl.ds(pl.multiple_of(step * rows + way * LANES + x * BLOCK, BLOCK), BLOCK)]

    staged = [0]

    def picks(dz_owner, dz_taker, offsets):
        takers = [node(dz_taker, o) for o in offsets]
        choice = choose(node(dz_owner, 0), takers)

        spots = []
        for o in offsets:
            local = dz_taker == 0 and o == 0
            spots.append(None if local else stage.at[pl.ds(staged[0] * BLOCK, BLOCK)])
            staged[0] += not local

        def send(src, step, way, piece):
            picked = jnp.dot(
                choice, src[:, part(piece)], preferred_element_type=jnp.float32).astype(jnp.bfloat16)
            for i, (taker, spot) in enumerate(zip(takers, spots)):
                block = picked[i * BLOCK:(i + 1) * BLOCK]
                there = slot(step, way).at[:, part(piece)]
                if spot is None:
                    there[...] = block
                    continue
                here = spot.at[:, part(piece)]
                here[...] = block
                copy(BLOCKS, slot_sem.at[step], here, there, dev=taker)

        return send

    loads[2].wait()
    pick_own = picks(0, 0, range(WIDE))
    pick_own(own, 0, 0, None)
    groups[pl.ds(LANES + 2 * BLOCK, 2 * BLOCK), :] = jnp.zeros((2 * BLOCK, width), jnp.bfloat16)

    ones = jnp.ones((rows, LANES), jnp.bfloat16)
    diagonal = lax.broadcasted_iota(jnp.int32, (rows, rows), 0) == lax.broadcasted_iota(
        jnp.int32, (rows, rows), 1)
    mine[...] = jnp.dot(
        jnp.where(diagonal, ids, 0.0).astype(jnp.bfloat16), ones, preferred_element_type=jnp.float32)

    in_plane_of = lax.broadcasted_iota(jnp.int32, (depth, members), 0) == lax.broadcasted_iota(
        jnp.int32, (depth, members), 1) // WIDE
    spread = lax.rem(lax.broadcasted_iota(jnp.int32, (members, LANES), 0), WIDE) == lax.broadcasted_iota(
        jnp.int32, (members, LANES), 1) // BLOCK
    my_row = pair[0, pl.ds(me, 1), :].astype(jnp.float32)
    ours_at[...] = jnp.dot(
        jnp.where(in_plane_of, my_row, 0.0).astype(jnp.bfloat16), spread.astype(jnp.bfloat16),
        preferred_element_type=jnp.float32)
    my_column = jnp.sum(
        jnp.where(lax.broadcasted_iota(jnp.int32, (members, members), 1) == me,
                  pair[0].astype(jnp.float32), 0.0), axis=1, keepdims=True)
    theirs_at[...] = jnp.dot(
        in_plane_of.astype(jnp.bfloat16), jnp.where(spread, my_column, 0.0).astype(jnp.bfloat16),
        preferred_element_type=jnp.float32)

    row_block = (lax.broadcasted_iota(jnp.int32, (rows, LANES), 0) // BLOCK).astype(jnp.float32)
    block_at = lax.broadcasted_iota(jnp.int32, (blocks, LANES), 0).astype(jnp.float32)

    def weigh(scores, topics, keep):
        factor = jnp.where(mine[...] == topics, 1.0, LEAKAGE)
        w = jnp.exp(scores * (SHARPNESS / width)) * factor
        return jnp.where(keep, w, 0.0).astype(jnp.bfloat16)

    def against(theirs, halves, first=False, last=False):
        scores = lax.dot_general(
            own[...], theirs, (((1,), (1,)), ((), ())), preferred_element_type=jnp.float32)
        ws = [
            weigh(scores[:, i * LANES:(i + 1) * LANES], topics, keep)
            for i, (topics, keep) in enumerate(halves)
        ]
        totals = sum(w.astype(jnp.float32) for w in ws)
        w = jnp.concatenate(ws, 1) if len(ws) > 1 else ws[0]
        sums = jnp.dot(w, theirs, preferred_element_type=jnp.float32)
        if first:
            acc[...] = sums
            weight_sum[...] = totals
        elif last:
            scale = 1.0 / jnp.sum(weight_sum[...] + totals, axis=1, keepdims=True)
            out[...] = ((acc[...] + sums) * scale).astype(out.dtype)
        else:
            acc[...] += sums
            weight_sum[...] += totals

    def plane_half(dz, plane):
        at = lax.rem(z + dz + depth, depth)
        theirs, ours = theirs_at[pl.ds(at, 1), :], ours_at[pl.ds(at, 1), :]
        topics = jnp.sum(jnp.where(block_at == theirs, planes[plane], 0.0), axis=0, keepdims=True)
        return topics, row_block == ours

    own_halves = []
    row_at = lax.broadcasted_iota(jnp.int32, (rows, LANES), 0)
    lane_at = lax.broadcasted_iota(jnp.int32, (rows, LANES), 1)
    for i in range(rows // LANES):
        topics = tile[pl.ds(i * WIDE, 1), :]
        for j in range(1, WIDE):
            topics = jnp.where(lane_part == j, tile[pl.ds(i * WIDE + j, 1), :], topics)
        own_halves.append((topics, row_at != lane_at + i * LANES))
    against(own[...], own_halves, first=True)

    await_bytes(tile_sem, parts.at[pl.ds(0, WIDE - 1)])
    plane = parts[0]
    for j in range(1, WIDE):
        plane = jnp.where(lane_part == j, parts[j], plane)
    planes[0] = plane

    def plane_at(way, hop):
        return 0 if hop == 0 else 2 * hop - 1 + way

    in_plane = {}

    def pass_plane(hop):
        for way in (0, 1):
            if hop:
                in_plane[way, hop].wait_recv()
            for further in (1, 2) if hop == hops and way == 0 else (1,):
                in_plane[way, hop + further] = copy(
                    TILES, plane_sem.at[way, hop + further - 1], planes.at[plane_at(way, hop)],
                    planes.at[plane_at(way, hop + further)], dev=node(further * (1 - 2 * way), 0))

    def finish(step):
        blocks_in = {0: WIDE - 1 + 2, far - 1: 2 * WIDE, far: WIDE}.get(step, 2 * (WIDE - 1))
        await_bytes(slot_sem.at[step], groups.at[pl.ds(step * rows, blocks_in * BLOCK)])
        if step == 0:
            await_bytes(slot_sem.at[far + 1], edges)
            topics = jnp.where(lane_part == 0, edges[0, pl.ds(blocks - 1, 1), :], edges[1, pl.ds(0, 1), :])
            before = jnp.where(slab > 0, 0.0, -1.0)
            behind = jnp.where(slab < slabs - 1, blocks - 1.0, -1.0)
            ours = jnp.where(lane_part == 0, before, jnp.where(lane_part == 1, behind, -1.0))
            halves = [plane_half(0, 0), (topics, row_block == ours)]
        elif step == far:
            in_plane[0, far].wait_recv()
            halves = [plane_half(-far, plane_at(0, far))]
        else:
            if step == far - 1:
                for way in (0, 1):
                    in_plane[way, step].wait_recv()
            halves = [plane_half(-step, plane_at(0, step)), plane_half(step, plane_at(1, step))]
        against(groups[pl.ds(step * rows, LANES * len(halves)), :], halves, last=step == far - 1)

    pass_plane(0)
    for hop in range(1, hops + 1):
        sends = []
        for way, offsets in ((0, (0, 1)), (1, (2, 3))):
            ring, by = rings[way * hops + hop - 1], 1 - 2 * way
            if hop == hops:
                sends.append((picks(-by * hop, by * 2, offsets), ring, far, 0))
                sends.append((picks(-by * hop, by, range(WIDE)), ring, far - 1, way))
        for way in (0, 1):
            ring, by = rings[way * hops + hop - 1], 1 - 2 * way
            sends.append((picks(-by * hop, 0, range(WIDE)), ring, hop, way))
        for piece in range(PIECES):
            if hop == 1 and piece == 1:
                pass_plane(hop)
            for way in (0, 1):
                in_ring[way, hop, piece].wait_recv()
                if hop < hops:
                    in_ring[way, hop + 1, piece] = ring_step(way, hop + 1, piece)
            if hop > 1 and piece == 0:
                pass_plane(hop)
            for send, ring, step, way in sends:
                if hop == hops:
                    send(ring, step, way, piece)
                elif piece == PIECES - 1:
                    send(ring, step, way, None)
        finish(hop - 1)
    finish(far)
    finish(hops)
    finish(far - 1)

    for way in (0, 1):
        await_bytes(send_sem.at[RING[way]], groups.at[pl.ds(0, hops * rows)])
    await_bytes(send_sem.at[BLOCKS], stage)
    await_bytes(send_sem.at[EDGES], groups.at[pl.ds(0, 2 * BLOCK)])
    await_bytes(send_sem.at[TILES], mine.at[pl.ds(0, tiles_sent[0] * blocks)])


def local(depth, slabs, embeddings, topic_ids, pair_blocks):
    rows, width = embeddings.shape
    hops = full_hops(depth)
    blocks = rows // BLOCK
    far = depth // 2
    whole = pltpu.VMEM((rows, width), jnp.bfloat16)
    ids = pltpu.VMEM((blocks, LANES), jnp.float32)
    return pl.pallas_call(
        functools.partial(kernel, depth, slabs),
        out_shape=pltpu.VMEM((rows, width), jnp.bfloat16),
        in_specs=[pl.BlockSpec(memory_space=pl.ANY)] * 3,
        out_specs=pl.BlockSpec(memory_space=pltpu.VMEM),
        scratch_shapes=[
            whole,
            pltpu.VMEM((1, rows), jnp.int32),
            pltpu.VMEM(pair_blocks.shape, jnp.int32),
            whole,
            pltpu.VMEM((far * rows + LANES, width), jnp.bfloat16),
            pltpu.VMEM((picked_blocks(depth) * BLOCK, width), jnp.bfloat16),
            ids,
            pltpu.VMEM((WIDE, blocks, LANES), jnp.float32),
            pltpu.VMEM((depth, blocks, LANES), jnp.float32),
            pltpu.VMEM((2, blocks, LANES), jnp.float32),
            pltpu.VMEM((rows, LANES), jnp.float32),
            pltpu.VMEM((depth, LANES), jnp.float32),
            pltpu.VMEM((depth, LANES), jnp.float32),
            pltpu.VMEM((rows, width), jnp.float32),
            pltpu.VMEM((rows, LANES), jnp.float32),
            pltpu.SemaphoreType.DMA((3,)),
            pltpu.SemaphoreType.DMA((5,)),
            pltpu.SemaphoreType.DMA((2, hops, PIECES)),
            pltpu.SemaphoreType.DMA((2, far)),
            pltpu.SemaphoreType.DMA((far + 2,)),
            pltpu.SemaphoreType.DMA,
        ] + [whole] * (2 * hops),
        compiler_params=pltpu.CompilerParams(
            collective_id=0, has_side_effects=True, vmem_limit_bytes=60 * 2**20),
    )(embeddings, topic_ids.reshape(1, rows), pair_blocks)


def solution(mesh):
    return jax.shard_map(
        functools.partial(local, mesh.shape["dev"] // WIDE, mesh.shape["topic"]),
        mesh=mesh,
        in_specs=(P(("topic", "dev"), None), P(("topic", "dev")), P("topic", None, None)),
        out_specs=P(("topic", "dev"), None),
        check_vma=False,
    )
```
